32 devices in a mesh: slab: 8 (over y, x, core), chan: 4 (over z).
Axes of the slice: x: 2, y: 2, z: 4, core: 2. Of those that a mesh axis runs over, the one named last changes fastest.
Arguments:
- field: bfloat16 [1, 128, 128, 128, 128], P(None, 'chan', 'slab'), may hold values from -6 to 6
- local_weight: bfloat16 [128, 128], replicated, may hold values from -0.5 to 0.5
- bias: float32 [128], replicated, may hold values from -3 to 3
- spec_weight: float32 [2, 128, 128, 4096], P(None, 'chan', None, 'slab'), may hold values from -4.2 to 4.2
Outputs:
- activated: bfloat16 [1, 128, 128, 128, 128], P(None, 'chan', 'slab')
The draws below stay inside these ranges and needn't reach their ends.
All inputs are finite; a program needn't handle non-finite values.
Results may differ from the reference program's by a relative error of at most 0.0026.
Values may be sent and summed in bfloat16 or wider, within the bound.
A program may use at most 384 MiB of HBM per device.

```python
import math
import jax
import jax.numpy as jnp
from jax import lax

GRID = 128
CHANNELS = 128
KEEP = 16
SAMPLES = 1
MODES = 4096


def block_scale(own_key, shape, pieces, least, top_value):
    loudness = 1.0
    for dim, blocks in pieces:
        draws = jax.random.uniform(jax.random.fold_in(jax.random.fold_in(own_key, 6), dim), (blocks,), jnp.float32, least / len(pieces), top_value / len(pieces))
        loudness = loudness * jnp.repeat(jnp.exp(draws), shape[dim] // blocks).reshape((-1,) + (1,) * (len(shape) - 1 - dim))
    return loudness


def scatter_about(key, shape, scale, most, split=(), kind=jnp.bfloat16):
    entries = jax.random.normal(key, shape, jnp.float32) * scale
    if len(split) > 0:
        entries = block_scale(key, shape, split, -0.22, 0.18) * entries
    return jnp.clip(entries, min=-most, max=most).astype(kind)


def setup_inputs(seed: int = 0) -> dict:
    arg_keys = jax.random.split(jax.random.key(seed), 5)
    field = scatter_about(arg_keys[0], (SAMPLES, CHANNELS, GRID, GRID, GRID), 1.0, 6.0, ((1, 4), (2, 8)))
    local_weight = scatter_about(arg_keys[1], (CHANNELS, CHANNELS), CHANNELS ** -0.5, 0.5)
    bias = scatter_about(arg_keys[2], (CHANNELS,), 0.5, 3.0, (), jnp.float32)
    spec_weight = scatter_about(arg_keys[3], (2, CHANNELS, CHANNELS, MODES), 0.7, 4.2, ((1, 4), (3, 8)), jnp.float32)
    return dict(field=field, local_weight=local_weight, bias=bias, spec_weight=spec_weight)


PRECISE = lax.Precision.HIGHEST


def mode_freqs(count, length):
    index = jnp.arange(count, dtype=jnp.int32)
    return jnp.where(index < count // 2, index, index + (length - count)).astype(jnp.int32)


def phase_table(freqs, positions, length):
    product_int = (freqs[:, None] * positions[None, :]) % length
    return 2.0 * math.pi * product_int.astype(jnp.float32) / length


def build_tables(zcells):
    xfreq = mode_freqs(KEEP, GRID)
    zfreq = jnp.arange(KEEP, dtype=jnp.int32)
    cells = jnp.arange(GRID, dtype=jnp.int32)
    angle_x = phase_table(xfreq, cells, GRID)
    angle_z = phase_table(zfreq, zcells, GRID)
    cos_x, sin_x = jnp.cos(angle_x), jnp.sin(angle_x)
    cos_z, sin_z = jnp.cos(angle_z), jnp.sin(angle_z)
    table_x = jnp.concatenate([cos_x, -sin_x], 0).astype(jnp.bfloat16)
    fold_factor = jnp.where(zfreq == 0, 1.0, 2.0).astype(jnp.float32)
    return cos_x, sin_x, cos_z, sin_z, table_x, fold_factor


def product(form, left, right):
    return jnp.einsum(form, left, right, precision=PRECISE)


def reference(field, local_weight, bias, spec_weight):
    cells = jnp.arange(GRID, dtype=jnp.int32)
    cos_x, sin_x, cos_z, sin_z, table_x, fold_factor = build_tables(cells)
    table_wide = table_x.astype(jnp.float32)
    weight_real, weight_imag = spec_weight[0], spec_weight[1]
    local_wide = local_weight.astype(jnp.float32)

    def one_sample(sample):
        section_x = product("kx,czxy->czky", table_wide, sample.astype(jnp.float32))
        part_real = section_x[:, :, :KEEP]
        part_imag = section_x[:, :, KEEP:]
        wave_real = product("czky,jy->czkj", part_real, cos_x) + product("czky,jy->czkj", part_imag, sin_x)
        wave_imag = product("czky,jy->czkj", part_imag, cos_x) - product("czky,jy->czkj", part_real, sin_x)
        four_real = product("czkj,lz->ckjl", wave_real, cos_z) + product("czkj,lz->ckjl", wave_imag, sin_z)
        four_imag = product("czkj,lz->ckjl", wave_imag, cos_z) - product("czkj,lz->ckjl", wave_real, sin_z)
        coef_real = four_real.reshape(CHANNELS, MODES)
        coef_imag = four_imag.reshape(CHANNELS, MODES)
        mixed_real = product("cm,ocm->om", coef_real, weight_real) - product("cm,ocm->om", coef_imag, weight_imag)
        mixed_imag = product("cm,ocm->om", coef_real, weight_imag) + product("cm,ocm->om", coef_imag, weight_real)
        spectral_real = mixed_real.reshape(CHANNELS, KEEP, KEEP, KEEP) * fold_factor
        spectral_imag = mixed_imag.reshape(CHANNELS, KEEP, KEEP, KEEP) * fold_factor
        plane_real = product("okjl,lz->ozkj", spectral_real, cos_z) - product("okjl,lz->ozkj", spectral_imag, sin_z)
        plane_imag = product("okjl,lz->ozkj", spectral_imag, cos_z) + product("okjl,lz->ozkj", spectral_real, sin_z)
        line_real = product("ozkj,kx->ozxj", plane_real, cos_x) - product("ozkj,kx->ozxj", plane_imag, sin_x)
        line_imag = product("ozkj,kx->ozxj", plane_imag, cos_x) + product("ozkj,kx->ozxj", plane_real, sin_x)

        def one_plane(inputs):
            plane, row_real, row_imag = inputs
            inverse = (product("oxj,jy->oxy", row_real, cos_x) - product("oxj,jy->oxy", row_imag, sin_x)) / (GRID ** 3)
            local = product("oc,cxy->oxy", local_wide, plane.astype(jnp.float32))
            total = inverse + local + bias[:, None, None]
            return jax.nn.gelu(total, approximate=False).astype(jnp.bfloat16)

        planes = lax.map(one_plane, (jnp.moveaxis(sample, 1, 0), jnp.moveaxis(line_real, 1, 0), jnp.moveaxis(line_imag, 1, 0)))
        return jnp.moveaxis(planes, 0, 1)

    return lax.map(one_sample, field)
```

```python
import math

import jax
import jax.numpy as jnp
from jax import lax
from jax.experimental import pallas as pl
from jax.experimental.pallas import tpu as pltpu
from jax.sharding import PartitionSpec as P

KEEP = 16
ROWS = 16
CHUNKS = (2, 2, 2, 2, 2, 2, 2, 1, 1)
WIDE_CHUNKS = 4

PRECISE = lax.Precision.HIGHEST


def mode_freqs(count, length):
    index = jnp.arange(count, dtype=jnp.int32)
    return jnp.where(index < count // 2, index, index + (length - count))


def phase_table(freqs, positions, length):
    product_int = freqs[:, None] * positions[None, :] % length
    return 2.0 * math.pi * product_int.astype(jnp.float32) / length


def product(form, left, right):
    return jnp.einsum(form, left, right, precision=PRECISE)


def map_kernel(kron_ref, own_ref, a_ref, b_ref, c_ref, mine_ref, part_ref):
    chans, _, xcells, ycells = own_ref.shape
    depth = chans * ROWS
    pair = 2 * ROWS

    @pl.loop(0, xcells // pair)
    def _(step):
        base = pl.multiple_of(step * pair, pair)
        total = None
        for index, ref in enumerate((own_ref, a_ref, b_ref, c_ref)):
            left = ref[:, 0, pl.ds(base, ROWS), :].reshape(depth, ycells)
            right = ref[:, 0, pl.ds(base + ROWS, ROWS), :].reshape(depth, ycells)
            block = jnp.concatenate([left, right], 1)
            term = jnp.dot(
                kron_ref[:, index * depth : (index + 1) * depth],
                block,
                preferred_element_type=jnp.float32,
            )
            total = term if total is None else total + term
        for half in range(2):
            piece = total[:, half * ycells : (half + 1) * ycells]
            piece = piece.reshape(2 * chans, ROWS, ycells)
            rows = pl.ds(base + half * ROWS, ROWS)
            mine_ref[:, 0, rows, :] = piece[:chans]
            part_ref[:, 0, rows, :] = piece[chans:].astype(part_ref.dtype)


def map_chunk(kron, field, others, start, depth, part_type):
    chans, _, xcells, ycells = field.shape
    block = (chans, 1, xcells, ycells)
    small = pl.BlockSpec(block, lambda z: (0, z, 0, 0))
    shape = (chans, depth, xcells, ycells)
    cost = 2 * 2 * kron.shape[0] * kron.shape[1] // 2 * depth * xcells * ycells // ROWS
    return pl.pallas_call(
        map_kernel,
        grid=(depth,),
        in_specs=[
            pl.BlockSpec(kron.shape, lambda z: (0, 0)),
            pl.BlockSpec(block, lambda z: (0, z + start, 0, 0)),
            small,
            small,
            small,
        ],
        out_specs=[small, small],
        out_shape=[
            jax.ShapeDtypeStruct(shape, jnp.float32),
            jax.ShapeDtypeStruct(shape, part_type),
        ],
        compiler_params=pltpu.CompilerParams(vmem_limit_bytes=44 * 2**20),
        cost_estimate=pl.CostEstimate(
            flops=cost, bytes_accessed=16 * chans * depth * xcells * ycells, transcendentals=0
        ),
        name="map_chunk",
    )(kron, field, *others)


def finish_kernel(table_ref, bias_ref, wave_ref, mine_ref, recv_ref, *rest):
    out_ref = rest[-1]
    table = table_ref[...]

    @pl.loop(0, out_ref.shape[0])
    def _(o):
        inverse = jnp.dot(table, wave_ref[o, 0], preferred_element_type=jnp.float32)
        total = inverse + (mine_ref[o, 0] + recv_ref[o, 0].astype(jnp.float32)) + bias_ref[o]
        value = 0.5 * total * (1.0 + lax.erf(total * (0.5**0.5)))
        out_ref[o, 0] = value.astype(out_ref.dtype)


def finish_chunk(table, bias, wave, mine, recv, out, start, whole_depth):
    chans, depth, xcells, ycells = mine.shape
    part = min(16, chans)
    block = (part, 1, xcells, ycells)
    small = pl.BlockSpec(block, lambda c, z: (c, z, 0, 0))
    placed = pl.BlockSpec(block, lambda c, z: (c, z + start, 0, 0))
    operands = [table, bias, wave, mine, recv]
    specs = [
        pl.BlockSpec(table.shape, lambda c, z: (0, 0)),
        pl.BlockSpec((part, 1, ycells), lambda c, z: (c, 0, 0)),
        pl.BlockSpec((part, 1, wave.shape[2], ycells), lambda c, z: (c, z + start, 0, 0)),
        small,
        small,
    ]
    aliases = {}
    if out is not None:
        aliases = {len(operands): 0}
        operands.append(out)
        specs.append(pl.BlockSpec(memory_space=pl.ANY))
    count = chans * depth * xcells * ycells
    return pl.pallas_call(
        finish_kernel,
        grid=(chans // part, depth),
        in_specs=specs,
        out_specs=placed,
        out_shape=jax.ShapeDtypeStruct((chans, whole_depth, xcells, ycells), jnp.bfloat16),
        input_output_aliases=aliases,
        compiler_params=pltpu.CompilerParams(vmem_limit_bytes=40 * 2**20),
        cost_estimate=pl.CostEstimate(
            flops=count * 60, bytes_accessed=count * 12, transcendentals=count
        ),
        name="finish_chunk",
    )(*operands)


def forward_modes(field, table_x, cos_yz, sin_yz):
    chans, zdepth, xcells, ycells = field.shape
    section = jnp.einsum("kx,czxy->ckzy", table_x, field, preferred_element_type=jnp.float32)
    section = section.reshape(chans * 2 * KEEP, zdepth * ycells)
    both = jnp.concatenate([cos_yz, -sin_yz], 1)
    four = jnp.dot(section, both, precision=PRECISE)
    four = four.reshape(chans, 2 * KEEP, 2, KEEP * KEEP)
    real = four[:, :KEEP, 0] - four[:, KEEP:, 1]
    imag = four[:, KEEP:, 0] + four[:, :KEEP, 1]
    return jnp.stack([real, imag], 0).transpose(2, 0, 1, 3)


def gather_line(value, axis, size):
    here = lax.axis_index(axis)
    pieces = jnp.zeros((size,) + value.shape, value.dtype)
    pieces = lax.dynamic_update_index_in_dim(pieces, value, here, 0)
    for shift in range(1, size):
        moved = lax.ppermute(value, axis, [(i, (i + shift) % size) for i in range(size)])
        pieces = lax.dynamic_update_index_in_dim(pieces, moved, (here + size - shift) % size, 0)
    return pieces


def mix(piece, spec_weight):
    chans = piece.shape[0] * piece.shape[3]
    coef = piece.transpose(2, 0, 3, 1, 4).reshape(2, chans, -1)
    weight_real, weight_imag = spec_weight[0], spec_weight[1]
    real = product("cm,ocm->om", coef[0], weight_real) - product("cm,ocm->om", coef[1], weight_imag)
    imag = product("cm,ocm->om", coef[0], weight_imag) + product("cm,ocm->om", coef[1], weight_real)
    return jnp.stack([real, imag], 0)


def on_device(slabs, lines, field, local_weight, bias, spec_weight):
    _, chans, zdepth, xcells, ycells = field.shape
    field = field[0]
    here = lax.axis_index("chan")
    zcells = lax.axis_index("slab") * zdepth + jnp.arange(zdepth, dtype=jnp.int32)
    freqs = mode_freqs(KEEP, xcells)
    zfreq = jnp.arange(KEEP, dtype=jnp.int32)
    angle_x = phase_table(freqs, jnp.arange(xcells, dtype=jnp.int32), xcells)
    angle_z = phase_table(zfreq, zcells, zdepth * slabs)
    cos_x, sin_x = jnp.cos(angle_x), jnp.sin(angle_x)
    cos_z, sin_z = jnp.cos(angle_z), jnp.sin(angle_z)
    table_x = jnp.concatenate([cos_x, -sin_x], 0).astype(jnp.bfloat16)
    fold = jnp.where(zfreq == 0, 1.0, 2.0).astype(jnp.float32)

    def joined(form, shape):
        def outer(z_part, y_part):
            return jnp.einsum(form, z_part, y_part, precision=PRECISE)

        cosine = outer(cos_z, cos_x) - outer(sin_z, sin_x)
        sine = outer(sin_z, cos_x) + outer(cos_z, sin_x)
        return cosine.reshape(shape), sine.reshape(shape)

    modes = KEEP * KEEP

    def local_parts():
        offset = lax.dynamic_slice_in_dim(bias, here * chans, chans, 0)
        return jnp.broadcast_to(offset[:, None, None], (chans, 1, ycells))

    bias_rows = local_parts()

    hubs = lines == 4
    if hubs:
        last = lines - 1
        partner = here + 1 - 2 * (here % 2)
        order = [here, last - here, partner, last - partner]

        def weight_block(out_block, in_block):
            return lax.dynamic_slice(
                local_weight, (out_block * chans, in_block * chans), (chans, chans)
            )

        top = jnp.concatenate([weight_block(here, block) for block in order], 1)
        low = [weight_block(partner, block) for block in order]
        low[2] = jnp.zeros_like(low[2])
        pair_weight = jnp.concatenate([top, jnp.concatenate(low, 1)], 0)
        eye = jnp.eye(ROWS, dtype=pair_weight.dtype)
        kron = (pair_weight[:, None, :, None] * eye[None, :, None, :]).reshape(
            2 * chans * ROWS, lines * chans * ROWS
        )
        swap = [(1, 2), (2, 1)]
        near = [(0, 1), (3, 2)]
        far = [(0, 2), (3, 1)]
        back = [(1, 0), (2, 3)]
        unit = zdepth // sum(CHUNKS)
        depths = [unit * depth for depth in CHUNKS]
        starts = [sum(depths[:i]) for i in range(len(depths))]
        arrived, parts = [], []
        for index, (start, depth) in enumerate(zip(starts, depths)):
            send = lax.slice_in_dim(field, start, start + depth, axis=1)
            if index >= 2:
                send, arrived[index - 2] = lax.optimization_barrier((send, arrived[index - 2]))
            arrived.append([lax.ppermute(send, "chan", pairs) for pairs in (swap, far, near)])
        for index, (start, depth) in enumerate(zip(starts, depths)):
            swapped, from_far, from_near = arrived[index]
            kind = jnp.float32 if index < WIDE_CHUNKS else jnp.bfloat16
            mine, part = map_chunk(
                kron, field, (swapped, from_near, from_far), start, depth, kind
            )
            parts.append((mine, lax.ppermute(part, "chan", back)))

    cos_yz, sin_yz = joined("lz,ky->zykl", (zdepth * ycells, modes))
    partial_value = forward_modes(field, table_x, cos_yz, sin_yz)
    owned = lax.psum_scatter(partial_value, "slab", scatter_dimension=0, tiled=True)
    piece = gather_line(owned, "chan", lines)
    mixed = mix(piece, spec_weight)
    spectrum = lax.all_gather(mixed, "slab", axis=0)
    spectrum = spectrum.reshape(slabs, 2, chans, KEEP // slabs, modes)
    spectrum = spectrum.transpose(2, 0, 3, 1, 4).reshape(chans * KEEP, 2 * modes)
    scale = 1.0 / (xcells * ycells * zdepth * slabs)
    cos_zy, sin_zy = joined("lz,ky->klzy", (KEEP, KEEP, zdepth * ycells))
    weight = (fold * scale)[None, :, None]
    cos_zy = (cos_zy * weight).reshape(modes, -1)
    sin_zy = (sin_zy * weight).reshape(modes, -1)
    back_table = jnp.concatenate(
        [jnp.concatenate([cos_zy, sin_zy], 1), jnp.concatenate([-sin_zy, cos_zy], 1)], 0
    )
    wave = jnp.dot(spectrum, back_table, precision=PRECISE)
    wave = wave.reshape(chans, KEEP, 2, zdepth, ycells).transpose(0, 3, 2, 1, 4)
    wave = wave.reshape(chans, zdepth, 2 * KEEP, ycells)
    wide_x = jnp.concatenate([cos_x, -sin_x], 0).T

    if hubs:
        high = lax.reduce_precision(wave, 8, 7)
        low_wave = (wave - high).astype(jnp.bfloat16)
        high = high.astype(jnp.bfloat16)
        waves = jnp.concatenate([high, low_wave, high], 2)
        high_x = lax.reduce_precision(wide_x, 8, 7)
        low_x = (wide_x - high_x).astype(jnp.bfloat16)
        high_x = high_x.astype(jnp.bfloat16)
        table = jnp.concatenate([high_x, high_x, low_x], 1)
        out = None
        for (mine, recv), start in zip(parts, starts):
            out = finish_chunk(table, bias_rows, waves, mine, recv, out, start, zdepth)
        return out[None]

    spread = lax.all_to_all(field, "chan", split_axis=2, concat_axis=0, tiled=True)
    mapped = jnp.einsum("oc,czxy->ozxy", local_weight, spread, preferred_element_type=jnp.float32)
    local = lax.all_to_all(mapped, "chan", split_axis=0, concat_axis=2, tiled=True)
    inverse = product("xk,ozky->ozxy", wide_x, wave)
    total = inverse + local + bias_rows[:, :, None]
    return jax.nn.gelu(total, approximate=False).astype(jnp.bfloat16)[None]


def solution(mesh):
    slabs, lines = mesh.shape["slab"], mesh.shape["chan"]
    placed = (P(None, "chan", "slab", None, None), P(), P(), P(None, "chan", None, "slab"))

    def body(field, local_weight, bias, spec_weight):
        return on_device(slabs, lines, field, local_weight, bias, spec_weight)

    return jax.shard_map(
        body,
        mesh=mesh,
        in_specs=placed,
        out_specs=P(None, "chan", "slab", None, None),
        check_vma=False,
    )
```
